32 devices in a mesh: cfg: 2 (over core), orbit: 8 (over z, y), tp: 2 (over x).
Axes of the slice: x: 2, y: 2, z: 4, core: 2. Of those that a mesh axis runs over, the one named last changes fastest.
Arguments:
- tokens: bfloat16 [2, 8, 1024, 1536], P('cfg', 'orbit', 'tp'), may hold values from -6 to 6
- modulation: float32 [2, 2, 1536], P('cfg'), may hold values from -2 to 6
- w_qkv: bfloat16 [1536, 3, 1536], P(None, None, 'tp'), may hold values from -1 to 1
- w_out: bfloat16 [1536, 1536], P('tp'), may hold values from -0.15625 to 0.15625
- adjacency: int32 [8, 4, 8], P('orbit'), may hold values 0 or 1
Outputs:
- guided: bfloat16 [8, 1024, 1536], P('orbit', 'tp', 'cfg')
The draws below stay inside these ranges and needn't reach their ends.
All inputs are finite; a program needn't handle non-finite values. No bound on the sum of `adjacency` on one device may be relied on, other than what follows from the above.
Results may differ from the reference program's by a relative error of at most 0.0075.
Values may be sent and summed in bfloat16 or wider, within the bound.
A program may use at most 128 MiB of HBM per device.

```python
import jax
import jax.numpy as jnp
from jax import lax

D = 1536
HEAD_DIM = 128
HEADS = 12
TOK_VIEW = 1024
BLOCK = 128
KEY_BLOCKS = 8
REACH = 2
VIEWS = 8


def draw_modulation(key, part):
    first = jax.random.fold_in(jax.random.fold_in(key, 11), 0)
    base = jnp.clip(jax.random.normal(first, (2, 2, D), jnp.float32) * 0.5, -2.0, 2.0)
    return base


def draw_w_qkv(key, part):
    first = jax.random.fold_in(jax.random.fold_in(key, 23), 0)
    spread = D ** (-0.5)
    return (jnp.clip(jax.random.normal(first, (D, 3, D), jnp.float32), -5.0, 5.0) * spread).astype(jnp.bfloat16)


def set_ends(drawn, stream_key, low, largest):
    extent = drawn.shape
    spot = [jax.random.randint(jax.random.fold_in(stream_key, axis), (), 0, extent[axis]) for axis in range(len(extent))]
    drawn = drawn.at[tuple(spot)].set(low)
    longest = extent.index(max(extent))
    spot[longest] = (spot[longest] + 1) % extent[longest]
    return drawn.at[tuple(spot)].set(largest)


def levels(key, dims, pieces, smallest, top_value):
    def one(axis_at, shards_of):
        steps = jax.random.uniform(jax.random.fold_in(jax.random.fold_in(key, 6), axis_at), (shards_of,), jnp.float32, smallest / len(pieces), top_value / len(pieces))
        return jnp.repeat(jnp.exp(steps), dims[axis_at] // shards_of).reshape((-1,) + (1,) * (len(dims) - axis_at - 1))

    gain = one(*pieces[0])
    for cut in pieces[1:]:
        gain = gain * one(*cut)
    return gain


def normal_values(stream_key, shape, scale, most, pieces=(), held_as=jnp.bfloat16):
    values = jax.random.normal(stream_key, shape, jnp.float32) * scale
    if len(pieces) > 0:
        values = levels(stream_key, shape, pieces, -0.22, 0.18) * values
    return jnp.clip(values, min=-most, max=most).astype(held_as)


def setup_inputs(seed: int = 0) -> dict:
    seeds = jax.random.split(jax.random.key(seed), 6)
    tokens = normal_values(seeds[0], (2, VIEWS, TOK_VIEW, D), 1.0, 6.0, ((0, 2), (1, 8), (2, 2)))
    modulation = draw_modulation(jax.random.fold_in(seeds[5], 71), 0)
    w_qkv = draw_w_qkv(jax.random.fold_in(seeds[5], 71), 0)
    w_out = normal_values(seeds[3], (D, D), D ** -0.5, 0.15625, ((0, 2),))
    adjacency = set_ends((jax.random.randint(seeds[4], (VIEWS, 2 * REACH, KEY_BLOCKS), 0, 4) < 3).astype(jnp.int32), jax.random.fold_in(seeds[4], 1), 0, 1)
    return {"tokens": tokens, "modulation": modulation, "w_qkv": w_qkv, "w_out": w_out, "adjacency": adjacency}


guide_scale = 4.0

def attend_head(queries, keyset, valueset, keymask):
    scores = jnp.dot(queries, keyset.T, preferred_element_type=jnp.float32) * queries.shape[1] ** (-0.5)
    scores = jnp.where(keymask[None, :], scores, -1e+30)
    peak = lax.optimization_barrier(jnp.max(scores, axis=1, keepdims=True))
    expon = jnp.exp(scores - peak)
    total = lax.optimization_barrier(jnp.sum(expon, axis=1, keepdims=True))
    weights = expon.astype(jnp.bfloat16)
    return (jnp.dot(weights, valueset, preferred_element_type=jnp.float32) / total).astype(jnp.bfloat16)

def reference(tokens, modulation, w_qkv, w_out, adjacency):
    flat_weight = w_qkv.reshape(D, 3 * D)

    def project(index):
        branch = index // VIEWS
        view = index % VIEWS
        inputs = tokens[branch, view].astype(jnp.float32)
        squares = lax.optimization_barrier(jnp.mean(inputs * inputs, axis=1, keepdims=True))
        shift_scale = modulation[branch]
        normed = (inputs * lax.rsqrt(squares + 1e-06) * (1.0 + shift_scale[1]) + shift_scale[0]).astype(jnp.bfloat16)
        return jnp.dot(normed, flat_weight, preferred_element_type=jnp.float32).astype(jnp.bfloat16).reshape(TOK_VIEW, 3, D)
    qkv_all = lax.map(project, jnp.arange(2 * VIEWS, dtype=jnp.int32))
    offsets = jnp.arange(-REACH, REACH + 1, dtype=jnp.int32)

    def attend_view(index):
        branch = index // VIEWS
        view = index % VIEWS
        queries = qkv_all[index, :, 0]
        neighbours = (view + offsets + VIEWS) % VIEWS
        gathered = qkv_all[branch * VIEWS + neighbours]
        keyflat = gathered[:, :, 1].reshape((2 * REACH + 1) * TOK_VIEW, D)
        valflat = gathered[:, :, 2].reshape((2 * REACH + 1) * TOK_VIEW, D)
        flags = adjacency[view]
        allowed = jnp.concatenate([flags[:REACH], jnp.ones((1, KEY_BLOCKS), jnp.int32), flags[REACH:]], axis=0)
        keymask = jnp.repeat(allowed, BLOCK, axis=1).reshape(-1) > 0

        def one_head(head_index):
            start = head_index * HEAD_DIM
            return attend_head(lax.dynamic_slice_in_dim(queries, start, HEAD_DIM, 1), lax.dynamic_slice_in_dim(keyflat, start, HEAD_DIM, 1), lax.dynamic_slice_in_dim(valflat, start, HEAD_DIM, 1), keymask)
        heads_out = lax.map(one_head, jnp.arange(HEADS, dtype=jnp.int32))
        context = jnp.transpose(heads_out, (1, 0, 2)).reshape(TOK_VIEW, D)
        return jnp.dot(context, w_out, preferred_element_type=jnp.float32).astype(jnp.bfloat16)
    branch_out = lax.map(attend_view, jnp.arange(2 * VIEWS, dtype=jnp.int32)).reshape(2, VIEWS, TOK_VIEW, D)
    guided = (1.0 - guide_scale) * branch_out[1].astype(jnp.float32) + guide_scale * branch_out[0].astype(jnp.float32)
    return guided.astype(jnp.bfloat16)
```

```python
import functools
import math

import jax
import jax.numpy as jnp
from jax import lax
from jax.experimental import pallas as pl
from jax.experimental.pallas import tpu as pltpu
from jax.sharding import PartitionSpec as P

HEAD_DIM = 128
REACH = 2
GUIDE = 4.0
MESH = pl.DeviceIdType.MESH
SLOTS = 2 * REACH + 1
TILE = 256
NEG = -1e30


def kernel(
    views,
    tok,
    mod,
    wq,
    wk,
    wv,
    wo,
    bias,
    out,
    xn,
    kv,
    q,
    acc,
    peak,
    wo_far,
    ctx,
    ctx_send,
    ctx_far,
    mix_send,
    mix_far,
    gather_sem,
    wo_sem,
    up_send,
    up_recv,
    down_send,
    down_recv,
    side_send,
    side_recv,
    relay_send,
    relay_recv,
    ctx_ssem,
    ctx_rsem,
    mix_sem,
):
    c = lax.axis_index("cfg")
    v = lax.axis_index("orbit")
    t = lax.axis_index("tp")
    half, width = xn.shape[1], xn.shape[2]
    heads = q.shape[0]
    chunks = 2 * heads
    odd = lax.rem(v, 2)
    mate = (c, v, 1 - t)
    up = (c, lax.rem(v + 2, views), t)
    down = (c, lax.rem(v + views - 2, views), t)
    side = (c, v + 1 - 2 * odd, t)
    core = (1 - c, v, t)

    barrier = pltpu.get_barrier_semaphore()
    for other in (mate, up, down, side, core):
        pl.semaphore_signal(barrier, inc=1, device_id=other, device_id_type=MESH)
    pl.semaphore_wait(barrier, 5)

    def remote(src, dst, ssem, rsem, dev):
        return pltpu.make_async_remote_copy(
            src_ref=src, dst_ref=dst, send_sem=ssem, recv_sem=rsem, device_id=dev, device_id_type=MESH
        )

    def up_copy(i):
        return remote(kv.at[0, i], kv.at[1, i], up_send.at[i], up_recv.at[i], up)

    def down_copy(i):
        return remote(kv.at[0, i], kv.at[2, i], down_send.at[i], down_recv.at[i], down)

    def side_copy(i):
        return remote(kv.at[0, i], kv.at[3, i], side_send.at[i], side_recv.at[i], side)

    def relay_copy(i):
        return remote(kv.at[2 - odd, i], kv.at[4, i], relay_send.at[i], relay_recv.at[i], side)

    def ctx_copy(n):
        cols = pl.ds(pl.multiple_of(n * HEAD_DIM, HEAD_DIM), HEAD_DIM)
        return remote(ctx_send.at[n], ctx_far.at[:, cols], ctx_ssem.at[n], ctx_rsem.at[n], mate)

    shift = mod[0:1, :]
    gain = 1.0 + mod[1:2, :]

    @pl.loop(0, half // 64)
    def _(r):
        rows = pl.ds(pl.multiple_of(r * 64, 64), 64)
        x = tok[rows, :].astype(jnp.float32)
        sq = jnp.mean(x * x, axis=1, keepdims=True)
        xn[0, rows, :] = (x * lax.rsqrt(sq + 1e-06) * gain + shift).astype(jnp.bfloat16)

    gather = remote(xn.at[0], xn.at[1], gather_sem.at[0], gather_sem.at[1], mate)
    gather.start()
    swap_wo = remote(wo, wo_far, wo_sem.at[0], wo_sem.at[1], mate)

    def project_kv(h, with_side):
        @pl.loop(0, heads)
        def _(n):
            cols = pl.ds(pl.multiple_of(n * HEAD_DIM, HEAD_DIM), HEAD_DIM)
            w = jnp.concatenate([wk[:, cols], wv[:, cols]], axis=1)
            i = h * heads + n

            r = jnp.dot(xn[h], w, preferred_element_type=jnp.float32).astype(jnp.bfloat16)
            kv[0, i, 0] = r[:, :HEAD_DIM]
            kv[0, i, 1] = r[:, HEAD_DIM:]
            up_copy(i).start()
            down_copy(i).start()
            if with_side:
                side_copy(i).start()

    def project_q(h):
        @pl.loop(0, heads // 2)
        def _(m):
            cols = pl.ds(pl.multiple_of(m * 2 * HEAD_DIM, 2 * HEAD_DIM), 2 * HEAD_DIM)
            r = jnp.dot(xn[h], wq[:, cols], preferred_element_type=jnp.float32)
            r = (r * (HEAD_DIM**-0.5 / math.log(2.0))).astype(jnp.bfloat16)
            rows = pl.ds(h * half, half)
            q[2 * m, rows, :] = r[:, :HEAD_DIM]
            q[2 * m + 1, rows, :] = r[:, HEAD_DIM:]

    project_kv(0, True)
    project_q(0)
    acc[...] = jnp.zeros_like(acc)
    peak[...] = jnp.full_like(peak, NEG)
    gather.wait_recv()
    project_kv(1, False)
    project_q(1)
    swap_wo.start()

    ones = jnp.ones((half, HEAD_DIM), jnp.bfloat16)

    def pass_on(i):
        up_copy(i).wait_recv()
        down_copy(i).wait_recv()
        relay_copy(i).start()

        @pl.when(i < heads)
        def _():
            side_copy(i + heads).start()

    pass_on(0)

    @pl.loop(0, chunks)
    def _(i):
        h = i // heads
        n = lax.rem(i, heads)

        @pl.when(i + 1 < chunks)
        def _():
            pass_on(i + 1)

        side_copy(i).wait_recv()
        relay_copy(i).wait_recv()

        @pl.loop(0, 2 * half // TILE)
        def _(r):
            rows = pl.ds(pl.multiple_of(r * TILE, TILE), TILE)
            queries = q[n, rows, :]
            scores = []
            for s in range(SLOTS):
                one = lax.dot_general(
                    queries,
                    kv[s, i, 0],
                    (((1,), (1,)), ((), ())),
                    preferred_element_type=jnp.float32,
                )
                if s > 0:
                    one = one + bias[s - 1, h]
                scores.append(one)
            top = scores[0]
            for s in range(1, SLOTS):
                top = jnp.maximum(top, scores[s])
            before = peak[n, rows, :1]
            now = jnp.maximum(before, jnp.max(top, axis=1, keepdims=True))
            total = acc[n, rows, :] * jnp.exp2(before - now)
            for s in range(SLOTS):
                weights = jnp.exp2(scores[s] - now).astype(jnp.bfloat16)
                total = total + jnp.dot(
                    weights,
                    jnp.concatenate([kv[s, i, 1], ones], axis=1),
                    preferred_element_type=jnp.float32,
                )
            acc[n, rows, :] = total
            peak[n, rows, :] = jnp.broadcast_to(now, (TILE, HEAD_DIM))

        @pl.when(h == 1)
        def _():
            def context(start):
                a = acc[n, pl.ds(start, half), :]
                return (a[:, :HEAD_DIM] / a[:, HEAD_DIM:]).astype(jnp.bfloat16)

            ctx_send[n] = context(half)
            ctx_copy(n).start()
            cols = pl.ds(pl.multiple_of(n * HEAD_DIM, HEAD_DIM), HEAD_DIM)
            ctx[:, cols] = context(0)

    swap_wo.wait_recv()
    for n in range(heads):
        ctx_copy(n).wait_recv()

    mine = pl.multiple_of(c * (width // 2), HEAD_DIM)
    others = pl.multiple_of((1 - c) * (width // 2), HEAD_DIM)

    def project_out(start, dst):
        @pl.loop(0, half // TILE)
        def _(r):
            rows = pl.ds(pl.multiple_of(r * TILE, TILE), TILE)
            cols = pl.ds(start, width // 2)
            y = jnp.dot(ctx[rows, :], wo[:, cols], preferred_element_type=jnp.float32)
            y = y + jnp.dot(ctx_far[rows, :], wo_far[:, cols], preferred_element_type=jnp.float32)
            dst[rows, :] = y.astype(jnp.bfloat16)

    project_out(others, mix_send)
    mix = remote(mix_send, mix_far, mix_sem.at[0], mix_sem.at[1], core)
    mix.start()
    project_out(mine, out)
    mix.wait_recv()
    own_scale = jnp.where(c == 0, GUIDE, 1.0 - GUIDE).astype(jnp.float32)

    @pl.loop(0, half // 64)
    def _(r):
        rows = pl.ds(pl.multiple_of(r * 64, 64), 64)
        a = out[rows, :].astype(jnp.float32) * own_scale
        b = mix_far[rows, :].astype(jnp.float32) * (1.0 - own_scale)
        out[rows, :] = (a + b).astype(jnp.bfloat16)

    gather.wait_send()
    swap_wo.wait_send()
    mix.wait_send()

    @pl.loop(0, chunks)
    def _(i):
        up_copy(i).wait_send()
        down_copy(i).wait_send()
        side_copy(i).wait_send()
        relay_copy(i).wait_send()

    @pl.loop(0, heads)
    def _(n):
        ctx_copy(n).wait_send()


def per_device(views, tokens, modulation, w_qkv, w_out, adjacency):
    tok = tokens[0, 0]
    half, width = tok.shape
    part = w_qkv.shape[2]
    heads = part // HEAD_DIM
    chunks = 2 * heads
    odd = lax.axis_index("orbit") % 2
    t = lax.axis_index("tp")
    flags = adjacency[0]
    near, far = flags[1], flags[2]
    order = jnp.stack(
        [flags[0], flags[3], jnp.where(odd == 1, near, far), jnp.where(odd == 1, far, near)]
    )
    keep = jnp.repeat(order, 2 * half // flags.shape[1], axis=1).reshape(4, 2, 1, half)
    keep = jnp.where(t == 0, keep, keep[:, ::-1])
    bias = jnp.where(keep > 0, 0.0, NEG).astype(jnp.float32)
    vmem = pl.BlockSpec(memory_space=pltpu.VMEM)
    bf16, f32 = jnp.bfloat16, jnp.float32
    dma = pltpu.SemaphoreType.DMA
    result = pl.pallas_call(
        functools.partial(kernel, views),
        out_shape=jax.ShapeDtypeStruct((half, width // 2), bf16),
        in_specs=[vmem] * 7,
        out_specs=vmem,
        scratch_shapes=[
            pltpu.VMEM((2, half, width), bf16),
            pltpu.VMEM((SLOTS, chunks, 2, half, HEAD_DIM), bf16),
            pltpu.VMEM((heads, 2 * half, HEAD_DIM), bf16),
            pltpu.VMEM((heads, 2 * half, 2 * HEAD_DIM), f32),
            pltpu.VMEM((heads, 2 * half, HEAD_DIM), f32),
            pltpu.VMEM((part, width), bf16),
            pltpu.VMEM((half, part), bf16),
            pltpu.VMEM((heads, half, HEAD_DIM), bf16),
            pltpu.VMEM((half, part), bf16),
            pltpu.VMEM((half, width // 2), bf16),
            pltpu.VMEM((half, width // 2), bf16),
            dma((2,)),
            dma((2,)),
        ]
        + [dma((chunks,))] * 8
        + [dma((heads,))] * 2
        + [dma((2,))],
        compiler_params=pltpu.CompilerParams(
            collective_id=0, has_side_effects=True, vmem_limit_bytes=62 * 1024 * 1024
        ),
        cost_estimate=pl.CostEstimate(
            flops=26_000_000_000, bytes_accessed=16_000_000, transcendentals=32_000_000
        ),
    )(tok, modulation[0], w_qkv[:, 0], w_qkv[:, 1], w_qkv[:, 2], w_out, bias)
    return result[None]


def solution(mesh):
    return jax.shard_map(
        functools.partial(per_device, mesh.shape["orbit"]),
        mesh=mesh,
        in_specs=(
            P("cfg", "orbit", "tp", None),
            P("cfg", None, None),
            P(None, None, "tp"),
            P("tp", None),
            P("orbit", None, None),
        ),
        out_specs=P("orbit", "tp", "cfg"),
        check_vma=False,
    )
```

```python
import functools
import math

import jax
import jax.numpy as jnp
from jax import lax
from jax.experimental import pallas as pl
from jax.experimental.pallas import tpu as pltpu
from jax.sharding import PartitionSpec as P

HEAD_DIM = 128
REACH = 2
GUIDE = 4.0
MESH = pl.DeviceIdType.MESH
SLOTS = 2 * REACH + 1
TILE = 256
NEG = -1e30


def kernel(
    views,
    tok,
    mod,
    w_all,
    wo,
    bias,
    out,
    xn,
    kv,
    q,
    acc,
    peak,
    wo_far,
    ctx,
    ctx_send,
    ctx_far,
    mix_send,
    mix_far,
    gather_sem,
    wo_sem,
    up_send,
    up_recv,
    down_send,
    down_recv,
    side_send,
    side_recv,
    relay_send,
    relay_recv,
    ctx_ssem,
    ctx_rsem,
    mix_sem,
):
    c = lax.axis_index("cfg")
    v = lax.axis_index("orbit")
    t = lax.axis_index("tp")
    half, width = xn.shape[1], xn.shape[2]
    heads = q.shape[0]
    chunks = 2 * heads
    odd = lax.rem(v, 2)
    mate = (c, v, 1 - t)
    up = (c, lax.rem(v + 2, views), t)
    down = (c, lax.rem(v + views - 2, views), t)
    side = (c, v + 1 - 2 * odd, t)
    core = (1 - c, v, t)

    barrier = pltpu.get_barrier_semaphore()
    for other in (mate, up, down, side, core):
        pl.semaphore_signal(barrier, inc=1, device_id=other, device_id_type=MESH)
    pl.semaphore_wait(barrier, 5)

    def remote(src, dst, ssem, rsem, dev):
        return pltpu.make_async_remote_copy(
            src_ref=src, dst_ref=dst, send_sem=ssem, recv_sem=rsem, device_id=dev, device_id_type=MESH
        )

    def up_copy(i):
        return remote(kv.at[0, i], kv.at[1, i], up_send.at[i], up_recv.at[i], up)

    def down_copy(i):
        return remote(kv.at[0, i], kv.at[2, i], down_send.at[i], down_recv.at[i], down)

    def side_copy(i):
        return remote(kv.at[0, i], kv.at[3, i], side_send.at[i], side_recv.at[i], side)

    def relay_copy(i):
        return remote(kv.at[2 - odd, i], kv.at[4, i], relay_send.at[i], relay_recv.at[i], side)

    def ctx_copy(n):
        cols = pl.ds(pl.multiple_of(n * HEAD_DIM, HEAD_DIM), HEAD_DIM)
        return remote(ctx_send.at[n], ctx_far.at[:, cols], ctx_ssem.at[n], ctx_rsem.at[n], mate)

    shift = mod[0:1, :]
    gain = 1.0 + mod[1:2, :]

    @pl.loop(0, half // 64)
    def _(r):
        rows = pl.ds(pl.multiple_of(r * 64, 64), 64)
        x = tok[rows, :].astype(jnp.float32)
        sq = jnp.mean(x * x, axis=1, keepdims=True)
        xn[0, rows, :] = (x * lax.rsqrt(sq + 1e-06) * gain + shift).astype(jnp.bfloat16)

    gather = remote(xn.at[0], xn.at[1], gather_sem.at[0], gather_sem.at[1], mate)
    gather.start()
    swap_wo = remote(wo, wo_far, wo_sem.at[0], wo_sem.at[1], mate)

    def project_kv(h, with_side):
        @pl.loop(0, heads)
        def _(n):
            cols = pl.ds(pl.multiple_of(n * HEAD_DIM, HEAD_DIM), HEAD_DIM)
            w = jnp.concatenate([w_all[1, :, cols], w_all[2, :, cols]], axis=1)
            i = h * heads + n

            r = jnp.dot(xn[h], w, preferred_element_type=jnp.float32).astype(jnp.bfloat16)
            kv[0, i, 0] = r[:, :HEAD_DIM]
            kv[0, i, 1] = r[:, HEAD_DIM:]
            up_copy(i).start()
            down_copy(i).start()
            if with_side:
                side_copy(i).start()

    def project_q(h):
        @pl.loop(0, heads // 2)
        def _(m):
            cols = pl.ds(pl.multiple_of(m * 2 * HEAD_DIM, 2 * HEAD_DIM), 2 * HEAD_DIM)
            r = jnp.dot(xn[h], w_all[0, :, cols], preferred_element_type=jnp.float32)
            r = (r * (HEAD_DIM**-0.5 / math.log(2.0))).astype(jnp.bfloat16)
            rows = pl.ds(h * half, half)
            q[2 * m, rows, :] = r[:, :HEAD_DIM]
            q[2 * m + 1, rows, :] = r[:, HEAD_DIM:]

    project_kv(0, True)
    project_q(0)
    acc[...] = jnp.zeros_like(acc)
    peak[...] = jnp.full_like(peak, NEG)
    gather.wait_recv()
    project_kv(1, False)
    project_q(1)
    swap_wo.start()

    ones = jnp.ones((half, HEAD_DIM), jnp.bfloat16)

    def pass_on(i):
        up_copy(i).wait_recv()
        down_copy(i).wait_recv()
        relay_copy(i).start()

        @pl.when(i < heads)
        def _():
            side_copy(i + heads).start()

    pass_on(0)

    @pl.loop(0, chunks)
    def _(i):
        h = i // heads
        n = lax.rem(i, heads)

        @pl.when(i + 1 < chunks)
        def _():
            pass_on(i + 1)

        side_copy(i).wait_recv()
        relay_copy(i).wait_recv()

        @pl.loop(0, 2 * half // TILE, unroll=4)
        def _(r):
            rows = pl.ds(pl.multiple_of(r * TILE, TILE), TILE)
            queries = q[n, rows, :]
            scores = []
            for s in range(SLOTS):
                one = lax.dot_general(
                    queries,
                    kv[s, i, 0],
                    (((1,), (1,)), ((), ())),
                    preferred_element_type=jnp.float32,
                )
                if s > 0:
                    one = one + bias[s - 1, h]
                scores.append(one)
            top = scores[0]
            for s in range(1, SLOTS):
                top = jnp.maximum(top, scores[s])
            before = peak[n, rows, :1]
            now = jnp.maximum(before, jnp.max(top, axis=1, keepdims=True))
            total = acc[n, rows, :] * jnp.exp2(before - now)
            for s in range(SLOTS):
                weights = jnp.exp2(scores[s] - now).astype(jnp.bfloat16)
                total = total + jnp.dot(
                    weights,
                    jnp.concatenate([kv[s, i, 1], ones], axis=1),
                    preferred_element_type=jnp.float32,
                )
            acc[n, rows, :] = total
            peak[n, rows, :] = jnp.broadcast_to(now, (TILE, HEAD_DIM))

        @pl.when(h == 1)
        def _():
            def context(start):
                a = acc[n, pl.ds(start, half), :]
                return (a[:, :HEAD_DIM] / a[:, HEAD_DIM:]).astype(jnp.bfloat16)

            ctx_send[n] = context(half)
            ctx_copy(n).start()
            cols = pl.ds(pl.multiple_of(n * HEAD_DIM, HEAD_DIM), HEAD_DIM)
            ctx[:, cols] = context(0)

    swap_wo.wait_recv()
    for n in range(heads):
        ctx_copy(n).wait_recv()

    mine = pl.multiple_of(c * (width // 2), HEAD_DIM)
    others = pl.multiple_of((1 - c) * (width // 2), HEAD_DIM)

    def project_out(start, dst):
        @pl.loop(0, half // TILE)
        def _(r):
            rows = pl.ds(pl.multiple_of(r * TILE, TILE), TILE)
            cols = pl.ds(start, width // 2)
            y = jnp.dot(ctx[rows, :], wo[:, cols], preferred_element_type=jnp.float32)
            y = y + jnp.dot(ctx_far[rows, :], wo_far[:, cols], preferred_element_type=jnp.float32)
            dst[rows, :] = y.astype(jnp.bfloat16)

    project_out(others, mix_send)
    mix = remote(mix_send, mix_far, mix_sem.at[0], mix_sem.at[1], core)
    mix.start()
    project_out(mine, out)
    mix.wait_recv()
    own_scale = jnp.where(c == 0, GUIDE, 1.0 - GUIDE).astype(jnp.float32)

    @pl.loop(0, half // 64)
    def _(r):
        rows = pl.ds(pl.multiple_of(r * 64, 64), 64)
        a = out[rows, :].astype(jnp.float32) * own_scale
        b = mix_far[rows, :].astype(jnp.float32) * (1.0 - own_scale)
        out[rows, :] = (a + b).astype(jnp.bfloat16)

    gather.wait_send()
    swap_wo.wait_send()
    mix.wait_send()

    @pl.loop(0, chunks)
    def _(i):
        up_copy(i).wait_send()
        down_copy(i).wait_send()
        side_copy(i).wait_send()
        relay_copy(i).wait_send()

    @pl.loop(0, heads)
    def _(n):
        ctx_copy(n).wait_send()


def per_device(views, tokens, modulation, w_qkv, w_out, adjacency):
    tok = tokens[0, 0]
    half, width = tok.shape
    part = w_qkv.shape[2]
    heads = part // HEAD_DIM
    chunks = 2 * heads
    odd = lax.axis_index("orbit") % 2
    t = lax.axis_index("tp")
    flags = adjacency[0]
    near, far = flags[1], flags[2]
    order = jnp.stack(
        [flags[0], flags[3], jnp.where(odd == 1, near, far), jnp.where(odd == 1, far, near)]
    )
    keep = jnp.repeat(order, 2 * half // flags.shape[1], axis=1).reshape(4, 2, 1, half)
    keep = jnp.where(t == 0, keep, keep[:, ::-1])
    bias = jnp.where(keep > 0, 0.0, NEG).astype(jnp.float32)
    vmem = pl.BlockSpec(memory_space=pltpu.VMEM)
    bf16, f32 = jnp.bfloat16, jnp.float32
    dma = pltpu.SemaphoreType.DMA
    result = pl.pallas_call(
        functools.partial(kernel, views),
        out_shape=jax.ShapeDtypeStruct((half, width // 2), bf16),
        in_specs=[vmem] * 5,
        out_specs=vmem,
        scratch_shapes=[
            pltpu.VMEM((2, half, width), bf16),
            pltpu.VMEM((SLOTS, chunks, 2, half, HEAD_DIM), bf16),
            pltpu.VMEM((heads, 2 * half, HEAD_DIM), bf16),
            pltpu.VMEM((heads, 2 * half, 2 * HEAD_DIM), f32),
            pltpu.VMEM((heads, 2 * half, HEAD_DIM), f32),
            pltpu.VMEM((part, width), bf16),
            pltpu.VMEM((half, part), bf16),
            pltpu.VMEM((heads, half, HEAD_DIM), bf16),
            pltpu.VMEM((half, part), bf16),
            pltpu.VMEM((half, width // 2), bf16),
            pltpu.VMEM((half, width // 2), bf16),
            dma((2,)),
            dma((2,)),
        ]
        + [dma((chunks,))] * 8
        + [dma((heads,))] * 2
        + [dma((2,))],
        compiler_params=pltpu.CompilerParams(
            collective_id=0, has_side_effects=True, vmem_limit_bytes=62 * 1024 * 1024
        ),
        cost_estimate=pl.CostEstimate(
            flops=26_000_000_000, bytes_accessed=16_000_000, transcendentals=32_000_000
        ),
    )(tok, modulation[0], jnp.transpose(w_qkv, (1, 0, 2)), w_out, bias)
    return result[None]


def solution(mesh):
    return jax.shard_map(
        functools.partial(per_device, mesh.shape["orbit"]),
        mesh=mesh,
        in_specs=(
            P("cfg", "orbit", "tp", None),
            P("cfg", None, None),
            P(None, None, "tp"),
            P("tp", None),
            P("orbit", None, None),
        ),
        out_specs=P("orbit", "tp", "cfg"),
        check_vma=False,
    )
```

```python
import functools
import math

import jax
import jax.numpy as jnp
from jax import lax
from jax.experimental import pallas as pl
from jax.experimental.pallas import tpu as pltpu
from jax.sharding import PartitionSpec as P

HEAD_DIM = 128
REACH = 2
GUIDE = 4.0
MESH = pl.DeviceIdType.MESH
SLOTS = 2 * REACH + 1
TILE = 256
NEG = -1e30


def kernel(
    views,
    tok,
    mod,
    w_hbm,
    wo_hbm,
    flags,
    out,
    w_all,
    wo,
    bias,
    partial,
    xn,
    kv,
    q,
    acc,
    peak,
    wo_far,
    ctx,
    ctx_send,
    ctx_far,
    mix_send,
    mix_far,
    gather_sem,
    wo_sem,
    up_send,
    up_recv,
    down_send,
    down_recv,
    side_send,
    side_recv,
    relay_send,
    relay_recv,
    ctx_ssem,
    ctx_rsem,
    mix_sem,
    load_sem,
):
    c = lax.axis_index("cfg")
    v = lax.axis_index("orbit")
    t = lax.axis_index("tp")
    half, width = xn.shape[1], xn.shape[2]
    heads = q.shape[0]
    chunks = 2 * heads
    odd = lax.rem(v, 2)
    mate = (c, v, 1 - t)
    up = (c, lax.rem(v + 2, views), t)
    down = (c, lax.rem(v + views - 2, views), t)
    side = (c, v + 1 - 2 * odd, t)
    core = (1 - c, v, t)

    barrier = pltpu.get_barrier_semaphore()
    for other in (mate, up, down, side, core):
        pl.semaphore_signal(barrier, inc=1, device_id=other, device_id_type=MESH)
    loads = [
        pltpu.make_async_copy(w_hbm.at[1], w_all.at[1], load_sem.at[0]),
        pltpu.make_async_copy(w_hbm.at[2], w_all.at[2], load_sem.at[1]),
        pltpu.make_async_copy(w_hbm.at[0], w_all.at[0], load_sem.at[2]),
        pltpu.make_async_copy(wo_hbm, wo, load_sem.at[3]),
    ]
    for load in loads:
        load.start()

    blocks = flags.shape[1]
    for s in range(SLOTS - 1):
        row = (0, REACH * 2 - 1, REACH - odd, REACH - 1 + odd)[s]
        for h in range(2):
            for b in range(blocks // 2):
                block = b + (blocks // 2) * lax.rem(h + t, 2)
                value = jnp.where(flags[row, block] > 0, 0.0, NEG).astype(jnp.float32)
                size = 2 * half // blocks
                bias[s, h, :, b * size : (b + 1) * size] = jnp.full((1, size), value, jnp.float32)

    def remote(src, dst, ssem, rsem, dev):
        return pltpu.make_async_remote_copy(
            src_ref=src, dst_ref=dst, send_sem=ssem, recv_sem=rsem, device_id=dev, device_id_type=MESH
        )

    def up_copy(i):
        return remote(kv.at[0, i], kv.at[1, i], up_send.at[i], up_recv.at[i], up)

    def down_copy(i):
        return remote(kv.at[0, i], kv.at[2, i], down_send.at[i], down_recv.at[i], down)

    def side_copy(i):
        return remote(kv.at[0, i], kv.at[3, i], side_send.at[i], side_recv.at[i], side)

    def relay_copy(i):
        return remote(kv.at[2 - odd, i], kv.at[4, i], relay_send.at[i], relay_recv.at[i], side)

    def ctx_copy(n):
        cols = pl.ds(pl.multiple_of(n * HEAD_DIM, HEAD_DIM), HEAD_DIM)
        return remote(ctx_send.at[n], ctx_far.at[:, cols], ctx_ssem.at[n], ctx_rsem.at[n], mate)

    shift = mod[0:1, :]
    gain = 1.0 + mod[1:2, :]

    @pl.loop(0, half // 64)
    def _(r):
        rows = pl.ds(pl.multiple_of(r * 64, 64), 64)
        x = tok[rows, :].astype(jnp.float32)
        sq = jnp.mean(x * x, axis=1, keepdims=True)
        xn[0, rows, :] = (x * lax.rsqrt(sq + 1e-06) * gain + shift).astype(jnp.bfloat16)

    pl.semaphore_wait(barrier, 5)
    gather = remote(xn.at[0], xn.at[1], gather_sem.at[0], gather_sem.at[1], mate)
    gather.start()
    swap_wo = remote(wo, wo_far, wo_sem.at[0], wo_sem.at[1], mate)

    def project_kv(h, with_side):
        @pl.loop(0, heads)
        def _(n):
            cols = pl.ds(pl.multiple_of(n * HEAD_DIM, HEAD_DIM), HEAD_DIM)
            w = jnp.concatenate([w_all[1, :, cols], w_all[2, :, cols]], axis=1)
            i = h * heads + n

            r = jnp.dot(xn[h], w, preferred_element_type=jnp.float32).astype(jnp.bfloat16)
            kv[0, i, 0] = r[:, :HEAD_DIM]
            kv[0, i, 1] = r[:, HEAD_DIM:]
            up_copy(i).start()
            down_copy(i).start()
            if with_side:
                side_copy(i).start()

    def project_q(h):
        @pl.loop(0, heads // 2)
        def _(m):
            cols = pl.ds(pl.multiple_of(m * 2 * HEAD_DIM, 2 * HEAD_DIM), 2 * HEAD_DIM)
            r = jnp.dot(xn[h], w_all[0, :, cols], preferred_element_type=jnp.float32)
            r = (r * (HEAD_DIM**-0.5 / math.log(2.0))).astype(jnp.bfloat16)
            rows = pl.ds(h * half, half)
            q[2 * m, rows, :] = r[:, :HEAD_DIM]
            q[2 * m + 1, rows, :] = r[:, HEAD_DIM:]

    loads[0].wait()
    loads[1].wait()
    project_kv(0, True)
    loads[2].wait()
    project_q(0)
    acc[...] = jnp.zeros_like(acc)
    peak[...] = jnp.full_like(peak, NEG)
    gather.wait_recv()
    project_kv(1, False)
    project_q(1)
    loads[3].wait()
    swap_wo.start()

    ones = jnp.ones((half, HEAD_DIM), jnp.bfloat16)

    def pass_on(i):
        up_copy(i).wait_recv()
        down_copy(i).wait_recv()
        relay_copy(i).start()

        @pl.when(i < heads)
        def _():
            side_copy(i + heads).start()

    pass_on(0)

    @pl.loop(0, chunks)
    def _(i):
        h = i // heads
        n = lax.rem(i, heads)

        @pl.when(i + 1 < chunks)
        def _():
            pass_on(i + 1)

        @pl.when(i + 1 == chunks)
        def _():
            swap_wo.wait_recv()
            for m in range(heads - 1):
                ctx_copy(m).wait_recv()
            known = (heads - 1) * HEAD_DIM

            @pl.loop(0, half // TILE)
            def _(r):
                rows = pl.ds(pl.multiple_of(r * TILE, TILE), TILE)
                for k in range(2):
                    cols = slice(k * (width // 2), (k + 1) * (width // 2))
                    y = jnp.dot(ctx[rows, :known], wo[:known, cols], preferred_element_type=jnp.float32)
                    partial[k, rows, :] = y + jnp.dot(
                        ctx_far[rows, :known], wo_far[:known, cols], preferred_element_type=jnp.float32
                    )

        side_copy(i).wait_recv()
        relay_copy(i).wait_recv()

        @pl.loop(0, 2 * half // TILE, unroll=4)
        def _(r):
            rows = pl.ds(pl.multiple_of(r * TILE, TILE), TILE)
            queries = q[n, rows, :]
            scores = []
            for s in range(SLOTS):
                one = lax.dot_general(
                    queries,
                    kv[s, i, 0],
                    (((1,), (1,)), ((), ())),
                    preferred_element_type=jnp.float32,
                )
                if s > 0:
                    one = one + bias[s - 1, h]
                scores.append(one)
            top = scores[0]
            for s in range(1, SLOTS):
                top = jnp.maximum(top, scores[s])
            before = peak[n, rows, :1]
            now = jnp.maximum(before, jnp.max(top, axis=1, keepdims=True))
            total = acc[n, rows, :] * jnp.exp2(before - now)
            for s in range(SLOTS):
                weights = jnp.exp2(scores[s] - now).astype(jnp.bfloat16)
                total = total + jnp.dot(
                    weights,
                    jnp.concatenate([kv[s, i, 1], ones], axis=1),
                    preferred_element_type=jnp.float32,
                )
            acc[n, rows, :] = total
            peak[n, rows, :] = jnp.broadcast_to(now, (TILE, HEAD_DIM))

        @pl.when(h == 1)
        def _():
            def context(start):
                a = acc[n, pl.ds(start, half), :]
                return (a[:, :HEAD_DIM] / a[:, HEAD_DIM:]).astype(jnp.bfloat16)

            ctx_send[n] = context(half)
            ctx_copy(n).start()
            cols = pl.ds(pl.multiple_of(n * HEAD_DIM, HEAD_DIM), HEAD_DIM)
            ctx[:, cols] = context(0)

    ctx_copy(heads - 1).wait_recv()
    mine = pl.multiple_of(c * (width // 2), HEAD_DIM)
    others = pl.multiple_of((1 - c) * (width // 2), HEAD_DIM)

    def project_out(k, start, dst):
        @pl.loop(0, half // TILE)
        def _(r):
            rows = pl.ds(pl.multiple_of(r * TILE, TILE), TILE)
            cols = pl.ds(start, width // 2)
            last = slice((heads - 1) * HEAD_DIM, heads * HEAD_DIM)
            y = jnp.dot(
                jnp.concatenate([ctx[rows, last], ctx_far[rows, last]], axis=1),
                jnp.concatenate([wo[last, cols], wo_far[last, cols]], axis=0),
                preferred_element_type=jnp.float32,
            )
            y = y + partial[k, rows, :]
            dst[rows, :] = y.astype(jnp.bfloat16)

    project_out(1 - c, others, mix_send)
    mix = remote(mix_send, mix_far, mix_sem.at[0], mix_sem.at[1], core)
    mix.start()
    project_out(c, mine, out)
    mix.wait_recv()
    own_scale = jnp.where(c == 0, GUIDE, 1.0 - GUIDE).astype(jnp.float32)

    @pl.loop(0, half // 64)
    def _(r):
        rows = pl.ds(pl.multiple_of(r * 64, 64), 64)
        a = out[rows, :].astype(jnp.float32) * own_scale
        b = mix_far[rows, :].astype(jnp.float32) * (1.0 - own_scale)
        out[rows, :] = (a + b).astype(jnp.bfloat16)

    gather.wait_send()
    swap_wo.wait_send()
    mix.wait_send()

    @pl.loop(0, chunks)
    def _(i):
        up_copy(i).wait_send()
        down_copy(i).wait_send()
        side_copy(i).wait_send()
        relay_copy(i).wait_send()

    @pl.loop(0, heads)
    def _(n):
        ctx_copy(n).wait_send()


def per_device(views, tokens, modulation, w_qkv, w_out, adjacency):
    tok = tokens[0, 0]
    half, width = tok.shape
    part = w_qkv.shape[2]
    heads = part // HEAD_DIM
    chunks = 2 * heads
    vmem = pl.BlockSpec(memory_space=pltpu.VMEM)
    anywhere = pl.BlockSpec(memory_space=pl.ANY)
    bf16, f32 = jnp.bfloat16, jnp.float32
    dma = pltpu.SemaphoreType.DMA
    result = pl.pallas_call(
        functools.partial(kernel, views),
        out_shape=jax.ShapeDtypeStruct((half, width // 2), bf16),
        in_specs=[vmem, vmem, anywhere, anywhere, pl.BlockSpec(memory_space=pltpu.SMEM)],
        out_specs=vmem,
        scratch_shapes=[
            pltpu.VMEM((3, width, part), bf16),
            pltpu.VMEM((part, width), bf16),
            pltpu.VMEM((SLOTS - 1, 2, 1, half), f32),
            pltpu.VMEM((2, half, width // 2), f32),
            pltpu.VMEM((2, half, width), bf16),
            pltpu.VMEM((SLOTS, chunks, 2, half, HEAD_DIM), bf16),
            pltpu.VMEM((heads, 2 * half, HEAD_DIM), bf16),
            pltpu.VMEM((heads, 2 * half, 2 * HEAD_DIM), f32),
            pltpu.VMEM((heads, 2 * half, HEAD_DIM), f32),
            pltpu.VMEM((part, width), bf16),
            pltpu.VMEM((half, part), bf16),
            pltpu.VMEM((heads, half, HEAD_DIM), bf16),
            pltpu.VMEM((half, part), bf16),
            pltpu.VMEM((half, width // 2), bf16),
            pltpu.VMEM((half, width // 2), bf16),
            dma((2,)),
            dma((2,)),
        ]
        + [dma((chunks,))] * 8
        + [dma((heads,))] * 2
        + [dma((2,)), dma((4,))],
        compiler_params=pltpu.CompilerParams(
            collective_id=0, has_side_effects=True, vmem_limit_bytes=62 * 1024 * 1024
        ),
        cost_estimate=pl.CostEstimate(
            flops=26_000_000_000, bytes_accessed=16_000_000, transcendentals=32_000_000
        ),
    )(tok, modulation[0], jnp.transpose(w_qkv, (1, 0, 2)), w_out, adjacency[0])
    return result[None]


def solution(mesh):
    return jax.shard_map(
        functools.partial(per_device, mesh.shape["orbit"]),
        mesh=mesh,
        in_specs=(
            P("cfg", "orbit", "tp", None),
            P("cfg", None, None),
            P(None, None, "tp"),
            P("tp", None),
            P("orbit", None, None),
        ),
        out_specs=P("orbit", "tp", "cfg"),
        check_vma=False,
    )
```
